512 devices in a mesh: grp: 16 (over y_hi, x), dev: 32 (over z, y_lo, core).
Axes of the slice: x: 4, y: 8 (y_hi: 4, y_lo: 2; y = y_hi * 2 + y_lo), z: 8, core: 2. Of those that a mesh axis runs over, the one named last changes fastest.
Arguments:
- amplitudes: float32 [16, 32, 8, 256, 256], P('grp', 'dev'), may hold values from -6 to 6
- joined_gates: float32 [3, 2, 256, 256], replicated, may hold values from -0.375 to 0.375
- pair_qubits: int32 [3, 8, 2], replicated, may hold values from 0 to 18, as said below
Outputs:
- final_state: float32 [16, 32, 8, 256, 256], P('grp', 'dev')
The draws below stay inside these ranges and needn't reach their ends.
Inputs may be any that keep to these rules, and one draw needn't show every extreme that they name: `pair_qubits`: in each layer the 16 qubit numbers are all different and are bits of the last three indices; every layer names both 0 and 18.
All inputs are finite; a program needn't handle non-finite values.
Results may differ from the reference program's by a relative error of at most 0.000098.
Values sent between devices are 32-bit elements; how exact they have to be, the bound alone decides.
A program may use at most 64 MiB of HBM per device.

```python
import jax
import jax.numpy as jnp
from jax import lax

GATE_BITS = 8
HIGH_BITS = 3
GATE = 256
HIGH = 8
LAYERS = 3
PAIRS = 8
GRPS = 16
DEVS = 32
MID_LOW = 8
LAST_LOW = 16


def draw_pair_qubits(key, part):
    key = jax.random.fold_in(key, 7)
    qubits = 2 * GATE_BITS + HIGH_BITS
    layer_keys = jax.random.split(key, LAYERS)

    def one_layer(layer_key):
        first_key, second_key = jax.random.split(layer_key)
        inner = jax.random.permutation(first_key, qubits - 2)[:2 * PAIRS - 2] + 1
        ends = jnp.array([0, qubits - 1], dtype=jnp.int32)
        chosen = jnp.concatenate([inner.astype(jnp.int32), ends])
        return jax.random.permutation(second_key, chosen)
    chosen = jax.vmap(one_layer)(layer_keys)
    return chosen.reshape(LAYERS, PAIRS, 2).astype(jnp.int32)


def steps_of(rng, extent, pieces, smallest, largest):
    loudness, own = 1.0, jax.random.fold_in(rng, 6)
    for dim, parts in pieces:
        heights = jnp.exp(jax.random.uniform(jax.random.fold_in(own, dim), (parts,), jnp.float32, smallest / len(pieces), largest / len(pieces)))
        loudness = loudness * jnp.repeat(heights, extent[dim] // parts).reshape([-1 if axis == dim else 1 for axis in range(len(extent))])
    return loudness


def centred(stream_key, dims, scale, bound, shards=(), held_as=jnp.bfloat16):
    drawn = jax.random.normal(stream_key, dims, jnp.float32) * scale
    if len(shards) > 0:
        drawn = steps_of(stream_key, dims, shards, -0.22, 0.18) * drawn
    return jnp.clip(drawn, min=-bound, max=bound).astype(held_as)


def setup_inputs(seed: int = 0) -> dict:
    key_list = jax.random.split(jax.random.key(seed), 4)
    amplitudes = centred(key_list[0], (GRPS, DEVS, HIGH, GATE, GATE), 1.0, 6.0, ((0, 16), (1, 32)), jnp.float32)
    joined_gates = centred(key_list[1], (LAYERS, 2, GATE, GATE), GATE ** -0.5, 0.375, (), jnp.float32)
    pair_qubits = draw_pair_qubits(jax.random.fold_in(key_list[3], 71), 0)
    return {"amplitudes": amplitudes, "joined_gates": joined_gates, "pair_qubits": pair_qubits}


def sign_of(flat_index, pair_row):
    parity = jnp.zeros_like(flat_index)
    for number in range(pair_row.shape[0]):
        bit_one = jnp.right_shift(flat_index, pair_row[number, 0])
        bit_two = jnp.right_shift(flat_index, pair_row[number, 1])
        parity = parity + (bit_one & bit_two & 1)
    return (1 - 2 * (parity & 1)).astype(jnp.float32)


def apply_layer_signs(current, pair_row):
    rows = GRPS * DEVS
    blocks = current.reshape(rows, HIGH, GATE, GATE)
    block_size = HIGH * GATE * GATE

    def one_block(inputs):
        block, row_index = inputs
        grid_shape = (HIGH, GATE, GATE)
        level_pos = lax.broadcasted_iota(jnp.int32, grid_shape, 0)
        middle = lax.broadcasted_iota(jnp.int32, grid_shape, 1)
        column = lax.broadcasted_iota(jnp.int32, grid_shape, 2)
        flat_index = row_index * block_size + (level_pos * GATE + middle) * GATE + column
        return block * sign_of(flat_index, pair_row)

    result = lax.map(one_block, (blocks, jnp.arange(rows, dtype=jnp.int32)))
    return result.reshape(current.shape)


def local_gates(current, pair_gates):
    highest = lax.Precision.HIGHEST
    current = jnp.einsum("ik,gdhkj->gdhij", pair_gates[0], current, precision=highest)
    return jnp.einsum("jk,gdhik->gdhij", pair_gates[1], current, precision=highest)


def global_gates(current, pair_gates):
    highest = lax.Precision.HIGHEST
    spread = current.reshape(GRPS, DEVS, HIGH, DEVS, MID_LOW, GRPS, LAST_LOW)
    middle_gate = pair_gates[0].reshape(DEVS, MID_LOW, DEVS, MID_LOW)
    last_gate = pair_gates[1].reshape(GRPS, LAST_LOW, GRPS, LAST_LOW)
    spread = jnp.einsum("pqrs,grhesfa->gpheqfa", middle_gate, spread, precision=highest)
    spread = jnp.einsum("pqrs,rdhebfs->pdhebfq", last_gate, spread, precision=highest)
    return spread.reshape(current.shape)


def reference(amplitudes, joined_gates, pair_qubits):
    current = apply_layer_signs(amplitudes, pair_qubits[0])
    current = local_gates(current, joined_gates[0])
    current = apply_layer_signs(current, pair_qubits[1])
    current = global_gates(current, joined_gates[1])
    current = apply_layer_signs(current, pair_qubits[2])
    current = local_gates(current, joined_gates[2])
    return current
```

```python
import functools

import jax
import jax.numpy as jnp
from jax import lax
from jax.sharding import PartitionSpec as P
import jax.experimental.pallas as pl
import jax.experimental.pallas.tpu as pltpu

MESH = pl.DeviceIdType.MESH
GRPS, DEVS = 16, 32
NODES = GRPS * DEVS
HIGH, GATE = 8, 256
NT = (((1,), (1,)), ((), ()))
NN = (((1,), (0,)), ((), ()))


def sign_of(flat, pairs, layer):
    parity = jnp.zeros_like(flat)
    for number in range(8):
        one = jnp.right_shift(flat, pairs[layer, number, 0])
        two = jnp.right_shift(flat, pairs[layer, number, 1])
        parity = parity ^ (one & two)
    return (1 - 2 * (parity & 1)).astype(jnp.float32)


def iota(shape, dim):
    return lax.broadcasted_iota(jnp.int32, shape, dim)


def split(values):
    high = values.astype(jnp.bfloat16)
    low = (values - high.astype(jnp.float32)).astype(jnp.bfloat16)
    return high, low


def split_gate(gate):
    high, low = split(gate)
    return jnp.concatenate([high, high, low], axis=1)


def gates_of(state, middle, last):
    high, low = split(state)
    wide = jnp.concatenate([high, low, high], axis=1)
    half = lax.dot_general(wide, last, NT, preferred_element_type=jnp.float32)
    high, low = split(half)
    tall = jnp.concatenate([high, low, high], axis=0)
    return lax.dot_general(middle, tall, NN, preferred_element_type=jnp.float32)


def regroup(tiles):
    group = iota((8, 128), 1) // 16
    tiles = [pltpu.roll(t, 16 * q, 1) if q else t for q, t in enumerate(tiles)]
    for bit in range(3):
        chosen = (group // 2**bit) % 2 == 1
        tiles = [jnp.where(chosen, tiles[(v + 2**bit) % 8], tiles[v]) for v in range(8)]
    return [pltpu.roll(tiles[8 - p], 128 - 16 * p, 1) if p else tiles[0] for p in range(8)]


def state_to_tiles(state, tiles, sign=None):
    def body(row, carry):
        for half in range(2):
            rows, cols = pl.ds(pl.multiple_of(row * 8, 8), 8), pl.ds(half * 128, 128)
            out = regroup([state[h, rows, cols] for h in range(8)])
            for p in range(8):
                tiles[(half * 8 + p) * DEVS + row] = out[p] if sign is None else out[p] * sign
        return carry

    lax.fori_loop(0, DEVS, body, 0)


def tiles_to_state(tiles, state, sign=None):
    def body(row, carry):
        for half in range(2):
            rows, cols = pl.ds(pl.multiple_of(row * 8, 8), 8), pl.ds(half * 128, 128)
            parts = [tiles[(half * 8 + p) * DEVS + row] for p in range(8)]
            out = regroup(parts if sign is None else [part * sign for part in parts])
            for h in range(8):
                state[h, rows, cols] = out[h]
        return carry

    lax.fori_loop(0, DEVS, body, 0)


def tile_sign(pairs, layer):
    e, f = lax.axis_index("dev"), lax.axis_index("grp")
    lane = iota((8, 128), 1)
    flat = (lane // 16) * 65536 + (e * 8 + iota((8, 128), 0)) * 256 + f * 16 + lane % 16
    return sign_of(flat, pairs, layer)


def first_kernel(pairs, gates, x, tiles, state, row_sign):
    middle, last = split_gate(gates[0, 0]), split_gate(gates[0, 1])
    base = sign_of(iota((GATE, GATE), 0) * 256 + iota((GATE, GATE), 1), pairs, 0)
    rows = iota((GATE, 128), 0) * 256
    row_sign[...] = sign_of((iota((GATE, 128), 1) % 8) * 65536 + rows, pairs, 0) * sign_of(rows, pairs, 0)
    level = iota((8, GATE), 0) * 65536
    column = iota((8, GATE), 1)
    col_sign = (
        sign_of(level + column, pairs, 0) * sign_of(column, pairs, 0) * sign_of(level, pairs, 0)
    )
    for h in range(8):
        signed = x[h] * base * row_sign[:, h : h + 1] * col_sign[h : h + 1, :]
        state[h] = gates_of(signed, middle, last)
    state_to_tiles(state, tiles)


def second_kernel(pairs, gates, got, tiles, state):
    middle, last = split_gate(gates[1, 0]), split_gate(gates[1, 1])
    tiles_to_state(got, state, tile_sign(pairs, 1))
    for h in range(8):
        state[h] = gates_of(state[h], middle, last)
    state_to_tiles(state, tiles, tile_sign(pairs, 2))


def third_kernel(pairs, gates, got, out, state):
    middle, last = split_gate(gates[2, 0]), split_gate(gates[2, 1])
    tiles_to_state(got, state)
    for h in range(8):
        out[h] = gates_of(state[h], middle, last)


def exchange_kernel(src, dst, send_sem, recv_sem, own_sem):
    grp, dev = lax.axis_index("grp"), lax.axis_index("dev")
    x, y, z, core = grp % 4, (grp // 4) * 2 + (dev // 2) % 2, dev // 4, dev % 2
    me = grp * DEVS + dev
    own = pltpu.make_async_copy(src.at[me], dst.at[me], own_sem)
    own.start()

    def body(step, carry):
        mixed = (step * 165) % NODES
        to_x = (x + mixed % 4) % 4
        to_y = (y + (mixed // 4) % 8) % 8
        to_z = (z + (mixed // 32) % 8) % 8
        to_core = (core + mixed // 256) % 2
        to_grp = (to_y // 2) * 4 + to_x
        to_dev = (to_z * 2 + to_y % 2) * 2 + to_core
        pltpu.make_async_remote_copy(
            src_ref=src.at[to_grp * DEVS + to_dev],
            dst_ref=dst.at[me],
            send_sem=send_sem,
            recv_sem=recv_sem,
            device_id=(to_grp, to_dev),
            device_id_type=MESH,
        ).start()
        return carry

    lax.fori_loop(1, NODES, body, 0)
    own.wait()
    others = pl.ds(0, NODES - 1)
    pltpu.make_async_remote_copy(
        src_ref=src.at[others],
        dst_ref=dst.at[others],
        send_sem=send_sem,
        recv_sem=recv_sem,
        device_id=((grp + 1) % GRPS, dev),
        device_id_type=MESH,
    ).wait()


VMEM = pl.BlockSpec(memory_space=pltpu.VMEM)
SMEM = pl.BlockSpec(memory_space=pltpu.SMEM)
TILES = jax.ShapeDtypeStruct((NODES, 8, 128), jnp.float32)
STATE = jax.ShapeDtypeStruct((HIGH, GATE, GATE), jnp.float32)


def compute(kernel, name, out, *scratch):
    return pl.pallas_call(
        kernel,
        out_shape=out,
        in_specs=[SMEM, VMEM, VMEM],
        out_specs=VMEM,
        scratch_shapes=[pltpu.VMEM((HIGH, GATE, GATE), jnp.float32), *scratch],
        name=name,
        compiler_params=pltpu.CompilerParams(vmem_limit_bytes=48 * 2**20),
    )


def exchange(tiles):
    return pl.pallas_call(
        exchange_kernel,
        out_shape=TILES,
        in_specs=[VMEM],
        out_specs=VMEM,
        scratch_shapes=[pltpu.SemaphoreType.DMA] * 3,
        name="exchange",
        compiler_params=pltpu.CompilerParams(
            has_side_effects=True, vmem_limit_bytes=48 * 2**20
        ),
    )(tiles)


def per_device(amplitudes, joined_gates, pair_qubits):
    state = amplitudes.reshape(HIGH, GATE, GATE)
    tiles = compute(first_kernel, "layer_one", TILES, pltpu.VMEM((GATE, 128), jnp.float32))(
        pair_qubits, joined_gates, state
    )
    tiles = exchange(tiles)
    tiles = compute(second_kernel, "layer_two", TILES)(pair_qubits, joined_gates, tiles)
    tiles = exchange(tiles)
    out = compute(third_kernel, "layer_three", STATE)(pair_qubits, joined_gates, tiles)
    return out.reshape(amplitudes.shape)


def solution(mesh):
    placed = (P("grp", "dev", None, None, None), P(), P())
    return jax.shard_map(
        per_device,
        mesh=mesh,
        in_specs=placed,
        out_specs=P("grp", "dev", None, None, None),
        check_vma=False,
    )
```

```python
import jax
import jax.numpy as jnp
from jax import lax
from jax.sharding import PartitionSpec as P
import jax.experimental.pallas as pl
import jax.experimental.pallas.tpu as pltpu

MESH = pl.DeviceIdType.MESH
GRPS, DEVS = 16, 32
NODES = GRPS * DEVS
HIGH, GATE = 8, 256
BLOCKS, BLOCK = 8, 64
NT = (((1,), (1,)), ((), ()))
NN = (((1,), (0,)), ((), ()))


def sign_of(flat, pairs, layer):
    parity = jnp.zeros_like(flat)
    for number in range(8):
        one = jnp.right_shift(flat, pairs[layer, 0, number])
        two = jnp.right_shift(flat, pairs[layer, 1, number])
        parity = parity ^ (one & two)
    return (1 - 2 * (parity & 1)).astype(jnp.float32)


def iota(shape, dim):
    return lax.broadcasted_iota(jnp.int32, shape, dim)


def split(values):
    high = values.astype(jnp.bfloat16)
    low = (values - high.astype(jnp.float32)).astype(jnp.bfloat16)
    return high, low


def split_gate(gate):
    high, low = split(gate)
    return jnp.concatenate([high, high, low], axis=1)


def by_last(state, last):
    high, low = split(state)
    wide = jnp.concatenate([high, low, high], axis=1)
    return lax.dot_general(wide, last, NT, preferred_element_type=jnp.float32)


def by_middle(middle, state):
    high, low = split(state)
    tall = jnp.concatenate([high, low, high], axis=0)
    return lax.dot_general(middle, tall, NN, preferred_element_type=jnp.float32)


def regroup(tiles):
    group = iota((8, 128), 1) // 16
    tiles = [pltpu.roll(t, 16 * q, 1) if q else t for q, t in enumerate(tiles)]
    for bit in range(3):
        chosen = (group // 2**bit) % 2 == 1
        tiles = [jnp.where(chosen, tiles[(v + 2**bit) % 8], tiles[v]) for v in range(8)]
    return [pltpu.roll(tiles[8 - p], 128 - 16 * p, 1) if p else tiles[0] for p in range(8)]


class Place:
    def __init__(self):
        self.grp, self.dev = lax.axis_index("grp"), lax.axis_index("dev")
        self.x, self.y = self.grp % 4, (self.grp // 4) * 2 + (self.dev // 2) % 2
        self.z, self.core = self.dev // 4, self.dev % 2
        self.me = self.grp * DEVS + self.dev

    def dev_of(self, block, step):
        z = (self.z + block // 4 + 2 * step) % 8
        low = (self.y + (block // 2) % 2) % 2
        return (z * 2 + low) * 2 + (self.core + block % 2) % 2

    def partner(self, block, step):
        mixed = (step * 27) % BLOCK
        x = (self.x + mixed % 4) % 4
        y = (self.y + (block // 2) % 2 + 2 * ((mixed // 4) % 4)) % 8
        z = (self.z + block // 4 + 2 * (mixed // 16)) % 8
        return (y // 2) * 4 + x, (z * 2 + y % 2) * 2 + (self.core + block % 2) % 2


def send_blocks(place, state, tiles, got, send_sem, recv_sem, sign=None):
    def block_body(block, carry):
        for step in range(4):
            dev = place.dev_of(block, step)
            rows = pl.ds(pl.multiple_of(dev * 8, 8), 8)
            for half in range(2):
                cols = pl.ds(half * 128, 128)
                out = regroup([state[h, rows, cols] for h in range(HIGH)])
                for p in range(8):
                    tile = out[p] if sign is None else out[p] * sign
                    tiles[(half * 8 + p) * DEVS + dev] = tile

        @pl.when(block == 0)
        def _():
            pltpu.make_async_copy(
                tiles.at[place.me], got.at[place.me], recv_sem.at[0]
            ).start()

        def send(step, inner):
            grp, dev = place.partner(block, step)
            pltpu.make_async_remote_copy(
                src_ref=tiles.at[grp * DEVS + dev],
                dst_ref=got.at[place.me],
                send_sem=send_sem,
                recv_sem=recv_sem.at[block],
                device_id=(grp, dev),
                device_id_type=MESH,
            ).start()
            return inner

        lax.fori_loop(jnp.where(block == 0, 1, 0), BLOCK, send, 0)
        return carry

    lax.fori_loop(0, BLOCKS, block_body, 0)


def take_blocks(place, got, staged, state, last, send_sem, recv_sem, sign=None):
    def block_body(block, carry):
        some = pl.ds(0, BLOCK)
        pltpu.make_async_remote_copy(
            src_ref=got.at[some],
            dst_ref=got.at[some],
            send_sem=send_sem,
            recv_sem=recv_sem.at[block],
            device_id=((place.grp + 1) % GRPS, place.dev),
            device_id_type=MESH,
        ).wait_recv()
        for step in range(4):
            dev = place.dev_of(block, step)
            for half in range(2):
                parts = [got[(half * 8 + p) * DEVS + dev] for p in range(8)]
                out = regroup(parts if sign is None else [part * sign for part in parts])
                for h in range(HIGH):
                    row = (step * HIGH + h) * 8
                    staged[row : row + 8, half * 128 : half * 128 + 128] = out[h]
        product = by_last(staged[...], last[...])
        for step in range(4):
            rows = pl.ds(pl.multiple_of(place.dev_of(block, step) * 8, 8), 8)
            for h in range(HIGH):
                row = (step * HIGH + h) * 8
                state[h, rows, :] = product[row : row + 8]
        return carry

    lax.fori_loop(0, BLOCKS, block_body, 0)


def window_kernel(
    pairs, gates, x, out,
    x_here, gates_here, wide, state, other, staged, row_sign,
    tiles_one, got_one, tiles_two, got_two,
    x_sem, gate_sem, out_sem, send_sem, recv_one, recv_two,
):
    place = Place()
    gate_copy = pltpu.make_async_copy(gates, gates_here, gate_sem)
    gate_copy.start()
    x_copies = [pltpu.make_async_copy(x.at[h], x_here.at[h], x_sem.at[h]) for h in range(HIGH)]
    for copy in x_copies:
        copy.start()

    barrier = pltpu.get_barrier_semaphore()

    def greet(step, carry):
        other_me = (place.me + step) % NODES
        pl.semaphore_signal(
            barrier, inc=1, device_id=(other_me // DEVS, other_me % DEVS), device_id_type=MESH
        )
        return carry

    lax.fori_loop(1, NODES, greet, 0)

    base = sign_of(iota((GATE, GATE), 0) * 256 + iota((GATE, GATE), 1), pairs, 0)
    rows = iota((GATE, 128), 0) * 256
    row_sign[...] = sign_of((iota((GATE, 128), 1) % 8) * 65536 + rows, pairs, 0) * sign_of(rows, pairs, 0)
    level = iota((8, GATE), 0) * 65536
    column = iota((8, GATE), 1)
    col_sign = (
        sign_of(level + column, pairs, 0) * sign_of(column, pairs, 0) * sign_of(level, pairs, 0)
    )

    gate_copy.wait()
    middle, last = split_gate(gates_here[0, 0]), split_gate(gates_here[0, 1])
    for h in range(HIGH):
        x_copies[h].wait()
        signed = x_here[h] * base * row_sign[:, h : h + 1] * col_sign[h : h + 1, :]
        state[h] = by_middle(middle, by_last(signed, last))

    pl.semaphore_wait(barrier, NODES - 1)
    send_blocks(place, state, tiles_one, got_one, send_sem.at[0], recv_one)

    for number, (layer, which) in enumerate(((1, 0), (1, 1), (2, 0), (2, 1))):
        wide[number] = split_gate(gates_here[layer, which])
    e, f = place.dev, place.grp
    lane = iota((8, 128), 1)
    flat = (lane // 16) * 65536 + (e * 8 + iota((8, 128), 0)) * 256 + f * 16 + lane % 16
    sign_one, sign_two = sign_of(flat, pairs, 1), sign_of(flat, pairs, 2)

    take_blocks(place, got_one, staged, other, wide.at[1], send_sem.at[0], recv_one, sign_one)
    for h in range(HIGH):
        state[h] = by_middle(wide[0], other[h])
    send_blocks(place, state, tiles_two, got_two, send_sem.at[1], recv_two, sign_two)
    take_blocks(place, got_two, staged, other, wide.at[3], send_sem.at[1], recv_two)
    out_copies = []
    for h in range(HIGH):
        x_here[h] = by_middle(wide[2], other[h])
        out_copies.append(pltpu.make_async_copy(x_here.at[h], out.at[h], out_sem.at[h]))
        out_copies[h].start()

    most = pl.ds(0, NODES - 1)
    for number, tiles in enumerate((tiles_one, tiles_two)):
        pltpu.make_async_remote_copy(
            src_ref=tiles.at[most],
            dst_ref=tiles.at[most],
            send_sem=send_sem.at[number],
            recv_sem=recv_one.at[0],
            device_id=((place.grp + 1) % GRPS, place.dev),
            device_id_type=MESH,
        ).wait_send()
    for copy in out_copies:
        copy.wait()


SMEM = pl.BlockSpec(memory_space=pltpu.SMEM)
ANY = pl.BlockSpec(memory_space=pl.ANY)
STATE = jax.ShapeDtypeStruct((HIGH, GATE, GATE), jnp.float32)


def per_device(amplitudes, joined_gates, pair_qubits):
    state = amplitudes.reshape(HIGH, GATE, GATE)
    held = pltpu.VMEM((HIGH, GATE, GATE), jnp.float32)
    tiles = pltpu.VMEM((NODES, 8, 128), jnp.float32)
    out = pl.pallas_call(
        window_kernel,
        out_shape=STATE,
        in_specs=[SMEM, ANY, ANY],
        out_specs=ANY,
        scratch_shapes=[
            held,
            pltpu.VMEM((3, 2, GATE, GATE), jnp.float32),
            pltpu.VMEM((4, GATE, 3 * GATE), jnp.bfloat16),
            held,
            held,
            pltpu.VMEM((GATE, GATE), jnp.float32),
            pltpu.VMEM((GATE, 128), jnp.float32),
            tiles,
            tiles,
            tiles,
            tiles,
            pltpu.SemaphoreType.DMA((HIGH,)),
            pltpu.SemaphoreType.DMA,
            pltpu.SemaphoreType.DMA((HIGH,)),
            pltpu.SemaphoreType.DMA((2,)),
            pltpu.SemaphoreType.DMA((BLOCKS,)),
            pltpu.SemaphoreType.DMA((BLOCKS,)),
        ],
        name="window",
        compiler_params=pltpu.CompilerParams(
            collective_id=0, has_side_effects=True, vmem_limit_bytes=56 * 2**20
        ),
        cost_estimate=pl.CostEstimate(flops=5 * 2**29, bytes_accessed=2**23, transcendentals=0),
    )(pair_qubits.transpose(0, 2, 1), joined_gates, state)
    return out.reshape(amplitudes.shape)


def solution(mesh):
    placed = (P("grp", "dev", None, None, None), P(), P())
    return jax.shard_map(
        per_device,
        mesh=mesh,
        in_specs=placed,
        out_specs=P("grp", "dev", None, None, None),
        check_vma=False,
    )
```

```python
import jax
import jax.numpy as jnp
from jax import lax
from jax.sharding import PartitionSpec as P
import jax.experimental.pallas as pl
import jax.experimental.pallas.tpu as pltpu

MESH = pl.DeviceIdType.MESH
GRPS, DEVS = 16, 32
NODES = GRPS * DEVS
HIGH, GATE = 8, 256
BLOCKS, BLOCK = 8, 64
NT = (((1,), (1,)), ((), ()))
NN = (((1,), (0,)), ((), ()))


def sign_of(flat, pairs, layer):
    parity = jnp.zeros_like(flat)
    for number in range(8):
        one = jnp.right_shift(flat, pairs[layer, 0, number])
        two = jnp.right_shift(flat, pairs[layer, 1, number])
        parity = parity ^ (one & two)
    return (1 - 2 * (parity & 1)).astype(jnp.float32)


def iota(shape, dim):
    return lax.broadcasted_iota(jnp.int32, shape, dim)


def split(values):
    high = values.astype(jnp.bfloat16)
    low = (values - high.astype(jnp.float32)).astype(jnp.bfloat16)
    return high, low


def split_gate(gate):
    high, low = split(gate)
    return jnp.concatenate([high, high, low], axis=1)


def by_last(state, last):
    high, low = split(state)
    wide = jnp.concatenate([high, low, high], axis=1)
    return lax.dot_general(wide, last, NT, preferred_element_type=jnp.float32)


def by_middle(middle, state):
    high, low = split(state)
    tall = jnp.concatenate([high, low, high], axis=0)
    return lax.dot_general(middle, tall, NN, preferred_element_type=jnp.float32)


def regroup(tiles):
    group = iota((8, 128), 1) // 16
    tiles = [pltpu.roll(t, 16 * q, 1) if q else t for q, t in enumerate(tiles)]
    for bit in range(3):
        chosen = (group // 2**bit) % 2 == 1
        tiles = [jnp.where(chosen, tiles[(v + 2**bit) % 8], tiles[v]) for v in range(8)]
    return [pltpu.roll(tiles[8 - p], 128 - 16 * p, 1) if p else tiles[0] for p in range(8)]


class Place:
    def __init__(self):
        self.grp, self.dev = lax.axis_index("grp"), lax.axis_index("dev")
        self.x, self.y = self.grp % 4, (self.grp // 4) * 2 + (self.dev // 2) % 2
        self.z, self.core = self.dev // 4, self.dev % 2
        self.me = self.grp * DEVS + self.dev

    def dev_of(self, block, step):
        odd, low, core = self.origin(block)
        return ((odd + 2 * step) * 2 + low) * 2 + core

    def origin(self, block):
        return (
            (self.z + block // 4) % 2,
            (self.y + (block // 2) % 2) % 2,
            (self.core + block % 2) % 2,
        )

    def partner(self, block, step):
        mixed = (step * 27) % BLOCK
        x = (self.x + mixed % 4) % 4
        y = (self.y + (block // 2) % 2 + 2 * ((mixed // 4) % 4)) % 8
        z = (self.z + block // 4 + 2 * (mixed // 16)) % 8
        return (y // 2) * 4 + x, (z * 2 + y % 2) * 2 + (self.core + block % 2) % 2


def send_blocks(place, state, tiles, got, send_sem, recv_sem, sign=None):
    def block_body(block, carry):
        for step in range(4):
            dev = place.dev_of(block, step)
            rows = pl.ds(pl.multiple_of(dev * 8, 8), 8)
            for half in range(2):
                cols = pl.ds(half * 128, 128)
                out = regroup([state[h, rows, cols] for h in range(HIGH)])
                for p in range(8):
                    tile = out[p] if sign is None else out[p] * sign
                    tiles[(half * 8 + p) * DEVS + dev] = tile

        @pl.when(block == 0)
        def _():
            pltpu.make_async_copy(
                tiles.at[place.me], got.at[place.me], recv_sem.at[0]
            ).start()

        def send(step, inner):
            grp, dev = place.partner(block, step)
            pltpu.make_async_remote_copy(
                src_ref=tiles.at[grp * DEVS + dev],
                dst_ref=got.at[place.me],
                send_sem=send_sem,
                recv_sem=recv_sem.at[block],
                device_id=(grp, dev),
                device_id_type=MESH,
            ).start()
            return inner

        lax.fori_loop(jnp.where(block == 0, 1, 0), BLOCK, send, 0)
        return carry

    lax.fori_loop(0, BLOCKS, block_body, 0)


def take_blocks(place, got, staged, state, last, send_sem, recv_sem, sign=None, done=None, done_sem=None):
    def block_body(block, carry):
        some = pl.ds(0, BLOCK)
        pltpu.make_async_remote_copy(
            src_ref=got.at[some],
            dst_ref=got.at[some],
            send_sem=send_sem,
            recv_sem=recv_sem.at[block],
            device_id=((place.grp + 1) % GRPS, place.dev),
            device_id_type=MESH,
        ).wait_recv()
        for step in range(4):
            dev = place.dev_of(block, step)
            for half in range(2):
                parts = [got[(half * 8 + p) * DEVS + dev] for p in range(8)]
                out = regroup(parts if sign is None else [part * sign for part in parts])
                for h in range(HIGH):
                    row = (step * HIGH + h) * 8
                    staged[row : row + 8, half * 128 : half * 128 + 128] = out[h]
        product = by_last(staged[...], last[...])
        if done is not None:
            odd, low, core = place.origin(block)
            number = (odd * 2 + low) * 2 + core
            state[number] = product
            pltpu.make_async_copy(state.at[number], done.at[number], done_sem).start()
            return carry
        for step in range(4):
            rows = pl.ds(pl.multiple_of(place.dev_of(block, step) * 8, 8), 8)
            for h in range(HIGH):
                row = (step * HIGH + h) * 8
                state[h, rows, :] = product[row : row + 8]
        return carry

    lax.fori_loop(0, BLOCKS, block_body, 0)


def window_kernel(
    pairs, gates, x, half_done,
    x_here, gates_here, wide, state, other, staged, row_sign,
    tiles_one, got_one, tiles_two, got_two,
    x_sem, gate_sem, out_sem, send_sem, recv_one, recv_two, ready,
):
    place = Place()
    gate_copy = pltpu.make_async_copy(gates, gates_here, gate_sem)
    gate_copy.start()
    x_copies = [pltpu.make_async_copy(x.at[h], x_here.at[h], x_sem.at[h]) for h in range(HIGH)]
    for copy in x_copies:
        copy.start()

    barrier = pltpu.get_barrier_semaphore()

    def greet_dev(step, carry):
        dev = (place.dev + step) % DEVS
        pl.semaphore_signal(barrier, inc=1, device_id=(place.grp, dev), device_id_type=MESH)
        return carry

    def greet_grp(step, carry):
        grp = (place.grp + step) % GRPS
        pl.semaphore_signal(barrier, inc=1, device_id=(grp, place.dev), device_id_type=MESH)
        return carry

    def say_ready(step, carry):
        grp = (place.grp + step) % GRPS
        pl.semaphore_signal(ready, inc=1, device_id=(grp, place.dev), device_id_type=MESH)
        return carry

    lax.fori_loop(1, DEVS, greet_dev, 0)
    lax.fori_loop(1, GRPS, greet_grp, 0)

    base = sign_of(iota((GATE, GATE), 0) * 256 + iota((GATE, GATE), 1), pairs, 0)
    rows = iota((GATE, 128), 0) * 256
    row_sign[...] = sign_of((iota((GATE, 128), 1) % 8) * 65536 + rows, pairs, 0) * sign_of(rows, pairs, 0)
    level = iota((8, GATE), 0) * 65536
    column = iota((8, GATE), 1)
    col_sign = (
        sign_of(level + column, pairs, 0) * sign_of(column, pairs, 0) * sign_of(level, pairs, 0)
    )

    gate_copy.wait()
    middle, last = split_gate(gates_here[0, 0]), split_gate(gates_here[0, 1])
    for h in range(HIGH):
        if h == 4:
            pl.semaphore_wait(barrier, DEVS + GRPS - 2)
            lax.fori_loop(1, GRPS, say_ready, 0)
        x_copies[h].wait()
        signed = x_here[h] * base * row_sign[:, h : h + 1] * col_sign[h : h + 1, :]
        state[h] = by_middle(middle, by_last(signed, last))

    pl.semaphore_wait(ready, GRPS - 1)
    send_blocks(place, state, tiles_one, got_one, send_sem.at[0], recv_one)

    for number, (layer, which) in enumerate(((1, 0), (1, 1), (2, 1))):
        wide[number] = split_gate(gates_here[layer, which])
    e, f = place.dev, place.grp
    lane = iota((8, 128), 1)
    flat = (lane // 16) * 65536 + (e * 8 + iota((8, 128), 0)) * 256 + f * 16 + lane % 16
    sign_one, sign_two = sign_of(flat, pairs, 1), sign_of(flat, pairs, 2)

    take_blocks(place, got_one, staged, other, wide.at[1], send_sem.at[0], recv_one, sign_one)
    for h in range(HIGH):
        state[h] = by_middle(wide[0], other[h])
    send_blocks(place, state, tiles_two, got_two, send_sem.at[1], recv_two, sign_two)
    take_blocks(
        place, got_two, staged, other, wide.at[2], send_sem.at[1], recv_two, None, half_done, out_sem
    )

    most = pl.ds(0, NODES - 1)
    for number, tiles in enumerate((tiles_one, tiles_two)):
        pltpu.make_async_remote_copy(
            src_ref=tiles.at[most],
            dst_ref=tiles.at[most],
            send_sem=send_sem.at[number],
            recv_sem=recv_one.at[0],
            device_id=((place.grp + 1) % GRPS, place.dev),
            device_id_type=MESH,
        ).wait_send()
    pltpu.make_async_copy(other, half_done, out_sem).wait()


def last_kernel(half_done, gates, out, half_here, gate_here, out_here, gate_sem, in_sem, out_sem):
    gate_copy = pltpu.make_async_copy(gates.at[2, 0], gate_here, gate_sem)
    gate_copy.start()
    half_copy = pltpu.make_async_copy(half_done, half_here, in_sem)
    half_copy.start()
    gate_copy.wait()
    middle = split_gate(gate_here[...])
    half_copy.wait()
    copies = []
    for h in range(HIGH):
        parts = []
        for dev in range(DEVS):
            z, low = dev // 4, dev % 4
            row = ((z // 2) * HIGH + h) * 8
            parts.append(half_here[(z % 2) * 4 + low, row : row + 8, :])
        out_here[h] = by_middle(middle, jnp.concatenate(parts, axis=0))
        copies.append(pltpu.make_async_copy(out_here.at[h], out.at[h], out_sem.at[h]))
        copies[h].start()
    for copy in copies:
        copy.wait()


SMEM = pl.BlockSpec(memory_space=pltpu.SMEM)
ANY = pl.BlockSpec(memory_space=pl.ANY)
STATE = jax.ShapeDtypeStruct((HIGH, GATE, GATE), jnp.float32)


def per_device(amplitudes, joined_gates, pair_qubits):
    state = amplitudes.reshape(HIGH, GATE, GATE)
    held = pltpu.VMEM((HIGH, GATE, GATE), jnp.float32)
    tiles = pltpu.VMEM((NODES, 8, 128), jnp.float32)
    half_done = pl.pallas_call(
        window_kernel,
        out_shape=STATE,
        in_specs=[SMEM, ANY, ANY],
        out_specs=ANY,
        scratch_shapes=[
            held,
            pltpu.VMEM((3, 2, GATE, GATE), jnp.float32),
            pltpu.VMEM((3, GATE, 3 * GATE), jnp.bfloat16),
            held,
            held,
            pltpu.VMEM((GATE, GATE), jnp.float32),
            pltpu.VMEM((GATE, 128), jnp.float32),
            tiles,
            tiles,
            tiles,
            tiles,
            pltpu.SemaphoreType.DMA((HIGH,)),
            pltpu.SemaphoreType.DMA,
            pltpu.SemaphoreType.DMA,
            pltpu.SemaphoreType.DMA((2,)),
            pltpu.SemaphoreType.DMA((BLOCKS,)),
            pltpu.SemaphoreType.DMA((BLOCKS,)),
            pltpu.SemaphoreType.REGULAR,
        ],
        name="window",
        compiler_params=pltpu.CompilerParams(
            collective_id=0, has_side_effects=True, vmem_limit_bytes=56 * 2**20
        ),
        cost_estimate=pl.CostEstimate(flops=5 * 2**29, bytes_accessed=2**23, transcendentals=0),
    )(pair_qubits.transpose(0, 2, 1), joined_gates, state)
    out = pl.pallas_call(
        last_kernel,
        out_shape=STATE,
        in_specs=[ANY, ANY],
        out_specs=ANY,
        scratch_shapes=[
            held,
            pltpu.VMEM((GATE, GATE), jnp.float32),
            held,
            pltpu.SemaphoreType.DMA,
            pltpu.SemaphoreType.DMA,
            pltpu.SemaphoreType.DMA((HIGH,)),
        ],
        name="last_product",
        compiler_params=pltpu.CompilerParams(vmem_limit_bytes=56 * 2**20),
    )(half_done, joined_gates)
    return out.reshape(amplitudes.shape)


def solution(mesh):
    placed = (P("grp", "dev", None, None, None), P(), P())
    return jax.shard_map(
        per_device,
        mesh=mesh,
        in_specs=placed,
        out_specs=P("grp", "dev", None, None, None),
        check_vma=False,
    )
```

```python
import jax
import jax.numpy as jnp
from jax import lax
from jax.sharding import PartitionSpec as P
import jax.experimental.pallas as pl
import jax.experimental.pallas.tpu as pltpu

MESH = pl.DeviceIdType.MESH
GRPS, DEVS, PAIRED = 16, 32, 16
CHIPS = GRPS * PAIRED
HIGH, HALF, GATE = 8, 4, 256
BLOCKS, BLOCK = 4, 64
NT = (((1,), (1,)), ((), ()))
NN = (((1,), (0,)), ((), ()))


def sign_of(flat, pairs, layer):
    parity = jnp.zeros_like(flat)
    for number in range(8):
        one = jnp.right_shift(flat, pairs[layer, 0, number])
        two = jnp.right_shift(flat, pairs[layer, 1, number])
        parity = parity ^ (one & two)
    return (1 - 2 * (parity & 1)).astype(jnp.float32)


def iota(shape, dim):
    return lax.broadcasted_iota(jnp.int32, shape, dim)


def split(values):
    high = values.astype(jnp.bfloat16)
    low = (values - high.astype(jnp.float32)).astype(jnp.bfloat16)
    return high, low


def split_gate(gate):
    high, low = split(gate)
    return jnp.concatenate([high, high, low], axis=1)


def by_last(state, last):
    high, low = split(state)
    wide = jnp.concatenate([high, low, high], axis=1)
    return lax.dot_general(wide, last, NT, preferred_element_type=jnp.float32)


def by_middle(middle, state):
    high, low = split(state)
    tall = jnp.concatenate([high, low, high], axis=0)
    return lax.dot_general(middle, tall, NN, preferred_element_type=jnp.float32)


def regroup(tiles):
    group = iota((8, 128), 1) // 16
    tiles = [pltpu.roll(t, 16 * q, 1) if q else t for q, t in enumerate(tiles)]
    for bit in range(3):
        chosen = (group // 2**bit) % 2 == 1
        tiles = [jnp.where(chosen, tiles[(v + 2**bit) % 8], tiles[v]) for v in range(8)]
    return [pltpu.roll(tiles[8 - p], 128 - 16 * p, 1) if p else tiles[0] for p in range(8)]


def pick(index, values):
    chosen = values[3]
    for number in (2, 1, 0):
        chosen = jnp.where(index == number, values[number], chosen)
    return chosen


class Place:
    def __init__(self):
        self.grp, self.dev = lax.axis_index("grp"), lax.axis_index("dev")
        self.x, self.y = self.grp % 4, (self.grp // 4) * 2 + (self.dev // 2) % 2
        self.z, self.core = self.dev // 4, self.dev % 2
        self.chip = self.grp * PAIRED + self.dev // 2
        self.sibling = (self.dev // 2) * 2 + 1 - self.core

    def paired(self, block, step):
        return ((self.z + block // 2) % 2 + 2 * step) * 2 + (self.y + block % 2) % 2

    def at(self, dx, dy, dz):
        x, y, z = (self.x + dx) % 4, (self.y + dy) % 8, (self.z + dz) % 8
        return (y // 2) * 4 + x, z * 2 + y % 2

    def partner(self, block, step, near_last):
        odd_z, odd_y = block // 2, block % 2
        mixed = (step * 27) % BLOCK
        dx, dy, dz = mixed % 4, 2 * ((mixed // 4) % 4), 2 * (mixed // 16)
        if near_last:
            far = (4, 2, 6, 0)
            last = block == 0
            dx = jnp.where(last, pick(step % 4, (2, 1, 3, 0)), dx)
            dy = jnp.where(last, pick((step // 4) % 4, far), dy)
            dz = jnp.where(last, pick(step // 16, far), dz)
        return self.at(dx, dy + odd_y, dz + odd_z)


def pack_block(place, half, block, state, tiles, sign=None):
    for step in range(4):
        paired = place.paired(block, step)
        for side in range(2):
            cols = pl.ds(side * 128, 128)
            parts = []
            for other in range(2):
                dev = paired * 2 + (place.core + other) % 2
                rows = pl.ds(pl.multiple_of(dev * 8, 8), 8)
                parts += [state[half * HALF + h, rows, cols] for h in range(HALF)]
            out = regroup(parts)
            for p in range(8):
                tile = out[p] if sign is None else out[p] * sign
                tiles[half, (side * 8 + p) * PAIRED + paired] = tile


def send_block(place, half, block, tiles, got, send_sem, recv_sem):
    def send(step, inner):
        grp, paired = place.partner(block, step, half == 1)
        chip = grp * PAIRED + paired

        @pl.when(chip != place.chip)
        def _():
            pltpu.make_async_remote_copy(
                src_ref=tiles.at[half, chip],
                dst_ref=got.at[half, place.chip],
                send_sem=send_sem,
                recv_sem=recv_sem.at[half * BLOCKS + block],
                device_id=(grp, paired * 2 + place.core),
                device_id_type=MESH,
            ).start()

        return inner

    lax.fori_loop(0, BLOCK, send, 0)


def keep_own(place, half, tiles, got, recv_sem):
    pltpu.make_async_copy(
        tiles.at[half, place.chip], got.at[half, place.chip], recv_sem.at[half * BLOCKS]
    ).start()


def send_half(place, half, state, tiles, got, send_sem, recv_sem, sign=None):
    def block_body(number, carry):
        block = BLOCKS - 1 - number
        pack_block(place, half, block, state, tiles, sign)
        send_block(place, half, block, tiles, got, send_sem, recv_sem)
        return carry

    lax.fori_loop(0, BLOCKS, block_body, 0)
    keep_own(place, half, tiles, got, recv_sem)


def take_half(
    place, half, got, state, last, mine, away, come, recv_sem, away_sem, come_sem, sign=None
):
    def keep(rows, block, core):
        product = by_last(rows, last[...])
        for step in range(4):
            dev = place.paired(block, step) * 2 + core
            where = pl.ds(pl.multiple_of(dev * 8, 8), 8)
            for h in range(HALF):
                row = (step * HALF + h) * 8
                state[half * HALF + h, where, :] = product[row : row + 8]

    def forward(block):
        slot = half * BLOCKS + block
        return pltpu.make_async_remote_copy(
            src_ref=away.at[slot],
            dst_ref=come.at[slot],
            send_sem=away_sem,
            recv_sem=come_sem.at[slot],
            device_id=(place.grp, place.sibling),
            device_id_type=MESH,
        )

    def keep_come(block):
        forward(block).wait_recv()
        keep(come[half * BLOCKS + block], block, 1 - place.core)

    def block_body(number, carry):
        block = BLOCKS - 1 - number
        slot = half * BLOCKS + block
        some = pl.ds(0, BLOCK)
        pltpu.make_async_copy(got.at[half, some], got.at[half, some], recv_sem.at[slot]).wait()
        for step in range(4):
            paired = place.paired(block, step)
            for side in range(2):
                cols = pl.ds(side * 128, 128)
                parts = [got[half, (side * 8 + p) * PAIRED + paired] for p in range(8)]
                out = regroup(parts if sign is None else [part * sign for part in parts])
                for h in range(HALF):
                    rows = pl.ds((step * HALF + h) * 8, 8)
                    mine[rows, cols] = out[h]
                    away[slot, rows, cols] = out[HALF + h]
        forward(block).start()
        keep(mine[...], block, place.core)

        @pl.when(number > 0)
        def _():
            keep_come(block + 1)

        return carry

    lax.fori_loop(0, BLOCKS, block_body, 0)
    keep_come(0)


def window_kernel(
    pairs, gates, x, half_done,
    x_here, gates_here, wide, state, other, mine, row_sign,
    tiles_one, got_one, tiles_two, got_two, away_one, come_one, away_two, come_two,
    x_sem, gate_sem, out_sem, send_sem, recv_one, recv_two, away_sem, come_sem_one, come_sem_two, ready,
):
    place = Place()

    barrier = pltpu.get_barrier_semaphore()

    def greet_plane(step, carry):
        grp, paired = place.at(step % 4, step // 4, 0)
        pl.semaphore_signal(
            barrier, inc=1, device_id=(grp, paired * 2 + place.core), device_id_type=MESH
        )
        return carry

    def tell_line(semaphore):
        def body(step, carry):
            grp, paired = place.at(0, 0, step)
            pl.semaphore_signal(
                semaphore, inc=1, device_id=(grp, paired * 2 + place.core), device_id_type=MESH
            )
            return carry

        lax.fori_loop(1, 8, body, 0)

    lax.fori_loop(1, 32, greet_plane, 0)
    tell_line(barrier)
    pl.semaphore_signal(
        barrier, inc=1, device_id=(place.grp, place.sibling), device_id_type=MESH
    )

    gate_copy = pltpu.make_async_copy(gates, gates_here, gate_sem)
    gate_copy.start()
    halves = [pl.ds(half * HALF, HALF) for half in range(2)]
    x_copies = [
        pltpu.make_async_copy(x.at[levels], x_here.at[levels], x_sem.at[half])
        for half, levels in enumerate(halves)
    ]
    for copy in x_copies:
        copy.start()

    base = sign_of(iota((GATE, GATE), 0) * 256 + iota((GATE, GATE), 1), pairs, 0)
    rows = iota((GATE, 128), 0) * 256
    row_sign[...] = sign_of((iota((GATE, 128), 1) % 8) * 65536 + rows, pairs, 0) * sign_of(rows, pairs, 0)
    level = iota((8, GATE), 0) * 65536
    column = iota((8, GATE), 1)
    col_sign = (
        sign_of(level + column, pairs, 0) * sign_of(column, pairs, 0) * sign_of(level, pairs, 0)
    )

    gate_copy.wait()
    middle, last = split_gate(gates_here[0, 0]), split_gate(gates_here[0, 1])

    def layer_one(half):
        x_copies[half].wait()
        for h in range(half * HALF, half * HALF + HALF):
            signed = x_here[h] * base * row_sign[:, h : h + 1] * col_sign[h : h + 1, :]
            state[h] = by_middle(middle, by_last(signed, last))

    def pack_body(block, carry):
        pack_block(place, 0, block, state, tiles_one)
        return carry

    def send_body(number, carry):
        send_block(place, 0, BLOCKS - 1 - number, tiles_one, got_one, send_sem.at[0], recv_one)
        return carry

    layer_one(0)
    pl.semaphore_wait(barrier, 31 + 7 + 1)
    tell_line(ready)
    lax.fori_loop(0, BLOCKS, pack_body, 0)
    layer_one(1)
    pl.semaphore_wait(ready, 7)
    lax.fori_loop(0, BLOCKS, send_body, 0)
    keep_own(place, 0, tiles_one, got_one, recv_one)
    send_half(place, 1, state, tiles_one, got_one, send_sem.at[0], recv_one)

    for number, (layer, which) in enumerate(((1, 0), (1, 1), (2, 0), (2, 1))):
        wide[number] = split_gate(gates_here[layer, which])
    lane = iota((8, 128), 1)
    levels, row = (lane // 16) % 4 * 65536, iota((8, 128), 0)
    column = place.grp * 16 + lane % 16
    both = (place.dev // 2) * 2 + (place.core + lane // 64) % 2
    arrives = levels + (both * 8 + row) * 256 + column
    leaves = levels + (place.dev * 8 + row) * 256 + column
    sign_one = [sign_of(arrives + half * HALF * 65536, pairs, 1) for half in range(2)]
    sign_two = [sign_of(leaves + half * HALF * 65536, pairs, 2) for half in range(2)]

    for half in range(2):
        take_half(
            place, half, got_one, other, wide.at[1], mine, away_one, come_one,
            recv_one, away_sem.at[0], come_sem_one, sign_one[half],
        )
        for h in range(half * HALF, half * HALF + HALF):
            state[h] = by_middle(wide[0], other[h])
        send_half(
            place, half, state, tiles_two, got_two, send_sem.at[1], recv_two, sign_two[half]
        )
    out_copies = []
    for half in range(2):
        take_half(
            place, half, got_two, other, wide.at[3], mine, away_two, come_two,
            recv_two, away_sem.at[1], come_sem_two,
        )
        source = other
        if half == 0:
            source = x_here
            for h in range(HALF):
                x_here[h] = by_middle(wide[2], other[h])
        out_copies.append(
            pltpu.make_async_copy(
                source.at[halves[half]], half_done.at[halves[half]], out_sem.at[half]
            )
        )
        out_copies[half].start()

    most = pl.ds(0, CHIPS - 1)
    for number, (tiles, away) in enumerate(((tiles_one, away_one), (tiles_two, away_two))):
        for half in range(2):
            part = tiles.at[half, most]
            pltpu.make_async_copy(part, part, send_sem.at[number]).wait()
        pltpu.make_async_copy(away, away, away_sem.at[number]).wait()
    for copy in out_copies:
        copy.wait()


def last_kernel(half_done, gates, out, half_here, gate_here, out_here, gate_sem, in_sem, out_sem):
    gate_copy = pltpu.make_async_copy(gates.at[2, 0], gate_here, gate_sem)
    gate_copy.start()
    copies = []
    for half in (1, 0):
        levels = pl.ds(half * HALF, HALF)
        copies.append(
            pltpu.make_async_copy(half_done.at[levels], half_here.at[levels], in_sem.at[half])
        )
        copies[-1].start()
    gate_copy.wait()
    middle = split_gate(gate_here[...])
    for copy in copies:
        copy.wait()
    finished = pl.ds(0, HALF)
    copies = [pltpu.make_async_copy(half_here.at[finished], out.at[finished], out_sem.at[0])]
    copies[0].start()
    for h in range(HALF):
        out_here[h] = by_middle(middle, half_here[HALF + h])
        copies.append(
            pltpu.make_async_copy(out_here.at[h], out.at[HALF + h], out_sem.at[1 + h])
        )
        copies[-1].start()
    for copy in copies:
        copy.wait()


SMEM = pl.BlockSpec(memory_space=pltpu.SMEM)
ANY = pl.BlockSpec(memory_space=pl.ANY)
STATE = jax.ShapeDtypeStruct((HIGH, GATE, GATE), jnp.float32)


def per_device(amplitudes, joined_gates, pair_qubits):
    state = amplitudes.reshape(HIGH, GATE, GATE)
    held = pltpu.VMEM((HIGH, GATE, GATE), jnp.float32)
    tiles = pltpu.VMEM((2, CHIPS, 8, 128), jnp.float32)
    within = pltpu.VMEM((2 * BLOCKS, 128, GATE), jnp.float32)
    dma = pltpu.SemaphoreType.DMA
    half_done = pl.pallas_call(
        window_kernel,
        out_shape=STATE,
        in_specs=[SMEM, ANY, ANY],
        out_specs=ANY,
        scratch_shapes=[
            held,
            pltpu.VMEM((3, 2, GATE, GATE), jnp.float32),
            pltpu.VMEM((4, GATE, 3 * GATE), jnp.bfloat16),
            held,
            held,
            pltpu.VMEM((128, GATE), jnp.float32),
            pltpu.VMEM((GATE, 128), jnp.float32),
            tiles,
            tiles,
            tiles,
            tiles,
            within,
            within,
            within,
            within,
            dma((2,)),
            dma,
            dma((2,)),
            dma((2,)),
            dma((2 * BLOCKS,)),
            dma((2 * BLOCKS,)),
            dma((2,)),
            dma((2 * BLOCKS,)),
            dma((2 * BLOCKS,)),
            pltpu.SemaphoreType.REGULAR,
        ],
        name="window",
        compiler_params=pltpu.CompilerParams(
            collective_id=0, has_side_effects=True, vmem_limit_bytes=56 * 2**20
        ),
        cost_estimate=pl.CostEstimate(flops=5 * 2**29, bytes_accessed=2**23, transcendentals=0),
    )(pair_qubits.transpose(0, 2, 1), joined_gates, state)
    out = pl.pallas_call(
        last_kernel,
        out_shape=STATE,
        in_specs=[ANY, ANY],
        out_specs=ANY,
        scratch_shapes=[
            held,
            pltpu.VMEM((GATE, GATE), jnp.float32),
            pltpu.VMEM((HALF, GATE, GATE), jnp.float32),
            dma,
            dma((2,)),
            dma((1 + HALF,)),
        ],
        name="last_product",
        compiler_params=pltpu.CompilerParams(vmem_limit_bytes=56 * 2**20),
    )(half_done, joined_gates)
    return out.reshape(amplitudes.shape)


def solution(mesh):
    placed = (P("grp", "dev", None, None, None), P(), P())
    return jax.shard_map(
        per_device,
        mesh=mesh,
        in_specs=placed,
        out_specs=P("grp", "dev", None, None, None),
        check_vma=False,
    )
```

```python
import jax
import jax.numpy as jnp
from jax import lax
from jax.sharding import PartitionSpec as P
import jax.experimental.pallas as pl
import jax.experimental.pallas.tpu as pltpu

MESH = pl.DeviceIdType.MESH
GRPS, DEVS, PAIRED = 16, 32, 16
CHIPS = GRPS * PAIRED
HIGH, HALF, GATE = 8, 4, 256
BLOCKS, BLOCK = 4, 64
NT = (((1,), (1,)), ((), ()))
NN = (((1,), (0,)), ((), ()))


def sign_of(flat, pairs, layer):
    parity = jnp.zeros_like(flat)
    for number in range(8):
        one = jnp.right_shift(flat, pairs[layer, 0, number])
        two = jnp.right_shift(flat, pairs[layer, 1, number])
        parity = parity ^ (one & two)
    return (1 - 2 * (parity & 1)).astype(jnp.float32)


def iota(shape, dim):
    return lax.broadcasted_iota(jnp.int32, shape, dim)


def split(values):
    high = values.astype(jnp.bfloat16)
    low = (values - high.astype(jnp.float32)).astype(jnp.bfloat16)
    return high, low


def split_gate(gate):
    high, low = split(gate)
    return jnp.concatenate([high, high, low], axis=1)


def by_last(state, last):
    high, low = split(state)
    wide = jnp.concatenate([high, low, high], axis=1)
    return lax.dot_general(wide, last, NT, preferred_element_type=jnp.float32)


def by_middle(middle, state):
    high, low = split(state)
    tall = jnp.concatenate([high, low, high], axis=0)
    return lax.dot_general(middle, tall, NN, preferred_element_type=jnp.float32)


def regroup(tiles):
    group = iota((8, 128), 1) // 16
    tiles = [pltpu.roll(t, 16 * q, 1) if q else t for q, t in enumerate(tiles)]
    for bit in range(3):
        chosen = (group // 2**bit) % 2 == 1
        tiles = [jnp.where(chosen, tiles[(v + 2**bit) % 8], tiles[v]) for v in range(8)]
    return [pltpu.roll(tiles[8 - p], 128 - 16 * p, 1) if p else tiles[0] for p in range(8)]


def pick(index, values):
    chosen = values[3]
    for number in (2, 1, 0):
        chosen = jnp.where(index == number, values[number], chosen)
    return chosen


class Place:
    def __init__(self):
        self.grp, self.dev = lax.axis_index("grp"), lax.axis_index("dev")
        self.x, self.y = self.grp % 4, (self.grp // 4) * 2 + (self.dev // 2) % 2
        self.z, self.core = self.dev // 4, self.dev % 2
        self.chip = self.grp * PAIRED + self.dev // 2
        self.sibling = (self.dev // 2) * 2 + 1 - self.core

    def paired(self, block, step):
        return ((self.z + block // 2) % 2 + 2 * step) * 2 + (self.y + block % 2) % 2

    def at(self, dx, dy, dz):
        x, y, z = (self.x + dx) % 4, (self.y + dy) % 8, (self.z + dz) % 8
        return (y // 2) * 4 + x, z * 2 + y % 2

    def partner(self, block, step, near_last):
        odd_z, odd_y = block // 2, block % 2
        mixed = (step * 27) % BLOCK
        dx, dy, dz = mixed % 4, 2 * ((mixed // 4) % 4), 2 * (mixed // 16)
        if near_last:
            far = (4, 2, 6, 0)
            last = block == 0
            dx = jnp.where(last, pick(step % 4, (2, 1, 3, 0)), dx)
            dy = jnp.where(last, pick((step // 4) % 4, far), dy)
            dz = jnp.where(last, pick(step // 16, far), dz)
        return self.at(dx, dy + odd_y, dz + odd_z)


def pack_block(place, half, block, state, tiles, sign=None):
    for step in range(4):
        paired = place.paired(block, step)
        for side in range(2):
            cols = pl.ds(side * 128, 128)
            parts = []
            for other in range(2):
                dev = paired * 2 + (place.core + other) % 2
                rows = pl.ds(pl.multiple_of(dev * 8, 8), 8)
                parts += [state[half * HALF + h, rows, cols] for h in range(HALF)]
            out = regroup(parts)
            for p in range(8):
                tile = out[p] if sign is None else out[p] * sign
                tiles[half, (side * 8 + p) * PAIRED + paired] = tile


def send_one(place, half, block, grp, paired, tiles, got, send_sem, recv_sem):
    pltpu.make_async_remote_copy(
        src_ref=tiles.at[half, grp * PAIRED + paired],
        dst_ref=got.at[half, place.chip],
        send_sem=send_sem,
        recv_sem=recv_sem.at[half * BLOCKS + block],
        device_id=(grp, paired * 2 + place.core),
        device_id_type=MESH,
    ).start()


def send_block(place, half, block, tiles, got, send_sem, recv_sem):
    def send(step, inner):
        grp, paired = place.partner(block, step, half == 1)

        @pl.when(grp * PAIRED + paired != place.chip)
        def _():
            send_one(place, half, block, grp, paired, tiles, got, send_sem, recv_sem)

        return inner

    lax.fori_loop(0, BLOCK, send, 0)


def keep_own(place, half, tiles, got, recv_sem):
    pltpu.make_async_copy(
        tiles.at[half, place.chip], got.at[half, place.chip], recv_sem.at[half * BLOCKS]
    ).start()


def send_half(place, half, state, tiles, got, send_sem, recv_sem, sign=None):
    def block_body(number, carry):
        block = BLOCKS - 1 - number
        pack_block(place, half, block, state, tiles, sign)
        send_block(place, half, block, tiles, got, send_sem, recv_sem)
        return carry

    lax.fori_loop(0, BLOCKS, block_body, 0)
    keep_own(place, half, tiles, got, recv_sem)


def take_half(
    place, half, got, state, first, last, mine, away, come, recv_sem, away_sem, come_sem, sign=None
):
    def keep(rows, block, core):
        product = by_last(rows, last[...])
        for step in range(4):
            dev = place.paired(block, step) * 2 + core
            where = pl.ds(pl.multiple_of(dev * 8, 8), 8)
            for h in range(HALF):
                row = (step * HALF + h) * 8
                state[first + h, where, :] = product[row : row + 8]

    def forward(block):
        slot = half * BLOCKS + block
        return pltpu.make_async_remote_copy(
            src_ref=away.at[slot],
            dst_ref=come.at[slot],
            send_sem=away_sem,
            recv_sem=come_sem.at[slot],
            device_id=(place.grp, place.sibling),
            device_id_type=MESH,
        )

    def keep_come(block):
        forward(block).wait_recv()
        keep(come[half * BLOCKS + block], block, 1 - place.core)

    def block_body(number, carry):
        block = BLOCKS - 1 - number
        slot = half * BLOCKS + block
        some = pl.ds(0, BLOCK)
        pltpu.make_async_copy(got.at[half, some], got.at[half, some], recv_sem.at[slot]).wait()
        for step in range(4):
            paired = place.paired(block, step)
            for side in range(2):
                cols = pl.ds(side * 128, 128)
                parts = [got[half, (side * 8 + p) * PAIRED + paired] for p in range(8)]
                out = regroup(parts if sign is None else [part * sign for part in parts])
                for h in range(HALF):
                    rows = pl.ds((step * HALF + h) * 8, 8)
                    mine[rows, cols] = out[h]
                    away[slot, rows, cols] = out[HALF + h]
        forward(block).start()
        keep(mine[...], block, place.core)

        @pl.when(number > 0)
        def _():
            keep_come(block + 1)

        return carry

    lax.fori_loop(0, BLOCKS, block_body, 0)
    keep_come(0)


def window_kernel(
    pairs, gates, x, first, second,
    x_here, gates_here, wide, state, other, mine, row_sign,
    tiles_one, got_one, tiles_two, got_two, away_one, come_one, away_two, come_two,
    x_sem, gate_sem, send_sem, recv_one, recv_two, away_sem, come_sem_one, come_sem_two, ready,
):
    place = Place()

    barrier = pltpu.get_barrier_semaphore()

    def greet_plane(step, carry):
        grp, paired = place.at(step % 4, step // 4, 0)
        pl.semaphore_signal(
            barrier, inc=1, device_id=(grp, paired * 2 + place.core), device_id_type=MESH
        )
        return carry

    def tell_line(semaphore):
        def body(step, carry):
            grp, paired = place.at(0, 0, step)
            pl.semaphore_signal(
                semaphore, inc=1, device_id=(grp, paired * 2 + place.core), device_id_type=MESH
            )
            return carry

        lax.fori_loop(1, 8, body, 0)

    lax.fori_loop(1, 32, greet_plane, 0)
    tell_line(barrier)
    pl.semaphore_signal(
        barrier, inc=1, device_id=(place.grp, place.sibling), device_id_type=MESH
    )

    gate_copy = pltpu.make_async_copy(gates, gates_here, gate_sem)
    gate_copy.start()
    halves = [pl.ds(half * HALF, HALF) for half in range(2)]
    x_copies = [
        pltpu.make_async_copy(x.at[levels], x_here.at[levels], x_sem.at[half])
        for half, levels in enumerate(halves)
    ]
    for copy in x_copies:
        copy.start()

    base = sign_of(iota((GATE, GATE), 0) * 256 + iota((GATE, GATE), 1), pairs, 0)
    rows = iota((GATE, 128), 0) * 256
    row_sign[...] = sign_of((iota((GATE, 128), 1) % 8) * 65536 + rows, pairs, 0) * sign_of(rows, pairs, 0)
    level = iota((8, GATE), 0) * 65536
    column = iota((8, GATE), 1)
    col_sign = (
        sign_of(level + column, pairs, 0) * sign_of(column, pairs, 0) * sign_of(level, pairs, 0)
    )

    gate_copy.wait()
    middle, last = split_gate(gates_here[0, 0]), split_gate(gates_here[0, 1])

    def layer_one(half):
        x_copies[half].wait()
        for h in range(half * HALF, half * HALF + HALF):
            signed = x_here[h] * base * row_sign[:, h : h + 1] * col_sign[h : h + 1, :]
            state[h] = by_middle(middle, by_last(signed, last))

    def pack_body(block, carry):
        pack_block(place, 0, block, state, tiles_one)
        return carry

    def send_body(number, carry):
        send_block(
            place, 0, BLOCKS - 1 - number, tiles_one, got_one, send_sem.at[0], recv_one
        )
        return carry

    layer_one(0)
    pl.semaphore_wait(barrier, 31 + 7 + 1)
    tell_line(ready)
    lax.fori_loop(0, BLOCKS, pack_body, 0)
    layer_one(1)
    pl.semaphore_wait(ready, 7)
    lax.fori_loop(0, BLOCKS, send_body, 0)
    keep_own(place, 0, tiles_one, got_one, recv_one)
    send_half(place, 1, state, tiles_one, got_one, send_sem.at[0], recv_one)

    for number, (layer, which) in enumerate(((1, 0), (1, 1), (2, 0), (2, 1))):
        wide[number] = split_gate(gates_here[layer, which])
    lane = iota((8, 128), 1)
    levels, row = (lane // 16) % 4 * 65536, iota((8, 128), 0)
    column = place.grp * 16 + lane % 16
    both = (place.dev // 2) * 2 + (place.core + lane // 64) % 2
    arrives = levels + (both * 8 + row) * 256 + column
    leaves = levels + (place.dev * 8 + row) * 256 + column
    sign_one = [sign_of(arrives + half * HALF * 65536, pairs, 1) for half in range(2)]
    sign_two = [sign_of(leaves + half * HALF * 65536, pairs, 2) for half in range(2)]

    for half in range(2):
        take_half(
            place, half, got_one, other, half * HALF, wide.at[1], mine, away_one, come_one,
            recv_one, away_sem.at[0], come_sem_one, sign_one[half],
        )
        for h in range(half * HALF, half * HALF + HALF):
            state[h] = by_middle(wide[0], other[h])
        send_half(
            place, half, state, tiles_two, got_two, send_sem.at[1], recv_two, sign_two[half]
        )
    for half, target in enumerate((first, second)):
        take_half(
            place, half, got_two, other, half * HALF, wide.at[3], mine, away_two, come_two,
            recv_two, away_sem.at[1], come_sem_two,
        )
        for h in range(HALF):
            target[h] = by_middle(wide[2], other[half * HALF + h])

    most = pl.ds(0, CHIPS - 1)
    for number, (tiles, away) in enumerate(((tiles_one, away_one), (tiles_two, away_two))):
        for half in range(2):
            part = tiles.at[half, most]
            pltpu.make_async_copy(part, part, send_sem.at[number]).wait()
        pltpu.make_async_copy(away, away, away_sem.at[number]).wait()


def leave_kernel(first, second, out, out_sem):
    copies = []
    for number, part in enumerate((first, second)):
        for piece in range(2):
            here = pl.ds(piece * 2, 2)
            there = pl.ds(number * HALF + piece * 2, 2)
            copies.append(
                pltpu.make_async_copy(part.at[here], out.at[there], out_sem.at[number * 2 + piece])
            )
            copies[-1].start()
    for copy in copies:
        copy.wait()


VMEM = pl.BlockSpec(memory_space=pltpu.VMEM)
SMEM = pl.BlockSpec(memory_space=pltpu.SMEM)
ANY = pl.BlockSpec(memory_space=pl.ANY)
STATE = jax.ShapeDtypeStruct((HIGH, GATE, GATE), jnp.float32)
PART = jax.ShapeDtypeStruct((HALF, GATE, GATE), jnp.float32)


def per_device(amplitudes, joined_gates, pair_qubits):
    state = amplitudes.reshape(HIGH, GATE, GATE)
    held = pltpu.VMEM((HIGH, GATE, GATE), jnp.float32)
    tiles = pltpu.VMEM((2, CHIPS, 8, 128), jnp.float32)
    within = pltpu.VMEM((2 * BLOCKS, 128, GATE), jnp.float32)
    dma = pltpu.SemaphoreType.DMA
    first, second = pl.pallas_call(
        window_kernel,
        out_shape=(PART, PART),
        in_specs=[SMEM, ANY, ANY],
        out_specs=(VMEM, VMEM),
        scratch_shapes=[
            held,
            pltpu.VMEM((3, 2, GATE, GATE), jnp.float32),
            pltpu.VMEM((4, GATE, 3 * GATE), jnp.bfloat16),
            held,
            held,
            pltpu.VMEM((128, GATE), jnp.float32),
            pltpu.VMEM((GATE, 128), jnp.float32),
            tiles,
            tiles,
            tiles,
            tiles,
            within,
            within,
            within,
            within,
            dma((2,)),
            dma,
            dma((2,)),
            dma((2 * BLOCKS,)),
            dma((2 * BLOCKS,)),
            dma((2,)),
            dma((2 * BLOCKS,)),
            dma((2 * BLOCKS,)),
            pltpu.SemaphoreType.REGULAR,
        ],
        name="window",
        compiler_params=pltpu.CompilerParams(
            collective_id=0, has_side_effects=True, vmem_limit_bytes=51 * 2**20
        ),
        cost_estimate=pl.CostEstimate(flops=5 * 2**29, bytes_accessed=2**23, transcendentals=0),
    )(pair_qubits.transpose(0, 2, 1), joined_gates, state)
    out = pl.pallas_call(
        leave_kernel,
        out_shape=STATE,
        in_specs=[VMEM, VMEM],
        out_specs=ANY,
        scratch_shapes=[dma((4,))],
        name="leave",
        compiler_params=pltpu.CompilerParams(vmem_limit_bytes=51 * 2**20),
    )(first, second)
    return out.reshape(amplitudes.shape)


def solution(mesh):
    placed = (P("grp", "dev", None, None, None), P(), P())
    return jax.shard_map(
        per_device,
        mesh=mesh,
        in_specs=placed,
        out_specs=P("grp", "dev", None, None, None),
        check_vma=False,
    )
```

```python
import jax
import jax.numpy as jnp
from jax import lax
from jax.sharding import PartitionSpec as P
import jax.experimental.pallas as pl
import jax.experimental.pallas.tpu as pltpu

MESH = pl.DeviceIdType.MESH
GRPS, DEVS, PAIRED = 16, 32, 16
CHIPS = GRPS * PAIRED
HIGH, HALF, GATE = 8, 4, 256
BLOCKS, BLOCK = 4, 64
NT = (((1,), (1,)), ((), ()))
NN = (((1,), (0,)), ((), ()))


def sign_of(flat, pairs, layer):
    parity = jnp.zeros_like(flat)
    for number in range(8):
        one = jnp.right_shift(flat, pairs[layer, 0, number])
        two = jnp.right_shift(flat, pairs[layer, 1, number])
        parity = parity ^ (one & two)
    return (1 - 2 * (parity & 1)).astype(jnp.float32)


def iota(shape, dim):
    return lax.broadcasted_iota(jnp.int32, shape, dim)


def split(values):
    high = values.astype(jnp.bfloat16)
    low = (values - high.astype(jnp.float32)).astype(jnp.bfloat16)
    return high, low


def split_gate(gate):
    high, low = split(gate)
    return jnp.concatenate([high, high, low], axis=1)


def by_last(state, last):
    high, low = split(state)
    wide = jnp.concatenate([high, low, high], axis=1)
    return lax.dot_general(wide, last, NT, preferred_element_type=jnp.float32)


def by_middle(middle, state):
    high, low = split(state)
    tall = jnp.concatenate([high, low, high], axis=0)
    return lax.dot_general(middle, tall, NN, preferred_element_type=jnp.float32)


def regroup(tiles):
    group = iota((8, 128), 1) // 16
    tiles = [pltpu.roll(t, 16 * q, 1) if q else t for q, t in enumerate(tiles)]
    for bit in range(3):
        chosen = (group // 2**bit) % 2 == 1
        tiles = [jnp.where(chosen, tiles[(v + 2**bit) % 8], tiles[v]) for v in range(8)]
    return [pltpu.roll(tiles[8 - p], 128 - 16 * p, 1) if p else tiles[0] for p in range(8)]


def pick(index, values):
    chosen = values[3]
    for number in (2, 1, 0):
        chosen = jnp.where(index == number, values[number], chosen)
    return chosen


class Place:
    def __init__(self):
        self.grp, self.dev = lax.axis_index("grp"), lax.axis_index("dev")
        self.x, self.y = self.grp % 4, (self.grp // 4) * 2 + (self.dev // 2) % 2
        self.z, self.core = self.dev // 4, self.dev % 2
        self.chip = self.grp * PAIRED + self.dev // 2
        self.sibling = (self.dev // 2) * 2 + 1 - self.core

    def paired(self, block, step):
        return ((self.z + block // 2) % 2 + 2 * step) * 2 + (self.y + block % 2) % 2

    def at(self, dx, dy, dz):
        x, y, z = (self.x + dx) % 4, (self.y + dy) % 8, (self.z + dz) % 8
        return (y // 2) * 4 + x, z * 2 + y % 2

    def partner(self, block, step, near_last):
        odd_z, odd_y = block // 2, block % 2
        mixed = (step * 27) % BLOCK
        dx, dy, dz = mixed % 4, 2 * ((mixed // 4) % 4), 2 * (mixed // 16)
        if near_last:
            far = (4, 2, 6, 0)
            last = block == 0
            dx = jnp.where(last, pick(step % 4, (2, 1, 3, 0)), dx)
            dy = jnp.where(last, pick((step // 4) % 4, far), dy)
            dz = jnp.where(last, pick(step // 16, far), dz)
        return self.at(dx, dy + odd_y, dz + odd_z)


def pack_block(place, half, block, state, tiles, sign=None):
    for step in range(4):
        paired = place.paired(block, step)
        for side in range(2):
            cols = pl.ds(side * 128, 128)
            parts = []
            for other in range(2):
                dev = paired * 2 + (place.core + other) % 2
                rows = pl.ds(pl.multiple_of(dev * 8, 8), 8)
                parts += [state[half * HALF + h, rows, cols] for h in range(HALF)]
            out = regroup(parts)
            for p in range(8):
                tile = out[p] if sign is None else out[p] * sign
                tiles[half, (side * 8 + p) * PAIRED + paired] = tile


def send_one(place, half, block, grp, paired, tiles, got, send_sem, recv_sem):
    pltpu.make_async_remote_copy(
        src_ref=tiles.at[half, grp * PAIRED + paired],
        dst_ref=got.at[half, place.chip],
        send_sem=send_sem,
        recv_sem=recv_sem.at[half * BLOCKS + block],
        device_id=(grp, paired * 2 + place.core),
        device_id_type=MESH,
    ).start()


def send_block(place, half, block, tiles, got, send_sem, recv_sem, near_last=False):
    def send(step, inner):
        grp, paired = place.partner(block, step, near_last)

        @pl.when(grp * PAIRED + paired != place.chip)
        def _():
            send_one(place, half, block, grp, paired, tiles, got, send_sem, recv_sem)

        return inner

    lax.fori_loop(0, BLOCK, send, 0)


def keep_own(place, half, tiles, got, recv_sem):
    pltpu.make_async_copy(
        tiles.at[half, place.chip], got.at[half, place.chip], recv_sem.at[half * BLOCKS]
    ).start()


def send_half(place, half, state, tiles, got, send_sem, recv_sem, sign=None, near_last=False):
    def block_body(number, carry):
        block = BLOCKS - 1 - number
        pack_block(place, half, block, state, tiles, sign)
        send_block(place, half, block, tiles, got, send_sem, recv_sem, near_last)
        return carry

    lax.fori_loop(0, BLOCKS, block_body, 0)
    keep_own(place, half, tiles, got, recv_sem)


def take_half(
    place, half, got, state, first, last, mine, away, come, recv_sem, away_sem, come_sem, sign=None
):
    def keep(rows, block, core):
        product = by_last(rows, last[...])
        for step in range(4):
            dev = place.paired(block, step) * 2 + core
            where = pl.ds(pl.multiple_of(dev * 8, 8), 8)
            for h in range(HALF):
                row = (step * HALF + h) * 8
                state[first + h, where, :] = product[row : row + 8]

    def forward(block):
        slot = half * BLOCKS + block
        return pltpu.make_async_remote_copy(
            src_ref=away.at[slot],
            dst_ref=come.at[slot],
            send_sem=away_sem,
            recv_sem=come_sem.at[slot],
            device_id=(place.grp, place.sibling),
            device_id_type=MESH,
        )

    def keep_come(block):
        forward(block).wait_recv()
        keep(come[half * BLOCKS + block], block, 1 - place.core)

    def block_body(number, carry):
        block = BLOCKS - 1 - number
        slot = half * BLOCKS + block
        some = pl.ds(0, BLOCK)
        pltpu.make_async_copy(got.at[half, some], got.at[half, some], recv_sem.at[slot]).wait()
        for step in range(4):
            paired = place.paired(block, step)
            for side in range(2):
                cols = pl.ds(side * 128, 128)
                parts = [got[half, (side * 8 + p) * PAIRED + paired] for p in range(8)]
                out = regroup(parts if sign is None else [part * sign for part in parts])
                for h in range(HALF):
                    rows = pl.ds((step * HALF + h) * 8, 8)
                    mine[rows, cols] = out[h]
                    away[slot, rows, cols] = out[HALF + h]
        forward(block).start()
        keep(mine[...], block, place.core)

        @pl.when(number > 0)
        def _():
            keep_come(block + 1)

        return carry

    lax.fori_loop(0, BLOCKS, block_body, 0)
    keep_come(0)


def window_kernel(
    pairs_there, gates, x, first, second,
    pairs, x_here, gates_here, wide, state, other, mine, row_sign,
    tiles_one, got_one, tiles_two, got_two, away_one, come_one, away_two, come_two,
    pair_sem, x_sem, gate_sem, send_sem, recv_one, recv_two, away_sem, come_sem_one, come_sem_two, ready,
):
    place = Place()
    pair_copy = pltpu.make_async_copy(pairs_there, pairs, pair_sem)
    pair_copy.start()

    barrier = pltpu.get_barrier_semaphore()

    def tell(semaphore, dx, dy, dz):
        grp, paired = place.at(dx, dy, dz)
        pl.semaphore_signal(
            semaphore, inc=1, device_id=(grp, paired * 2 + place.core), device_id_type=MESH
        )

    def tell_line(semaphore):
        for dz in (4, 3, 5, 2, 6, 1, 7):
            tell(semaphore, 0, 0, dz)

    plane = [(dx, dy) for dx in range(4) for dy in range(8) if dx + dy > 0]
    plane.sort(key=lambda at: -min(at[0], 4 - at[0]) - min(at[1], 8 - at[1]))
    for dx, dy in plane:
        tell(barrier, dx, dy, 0)
    tell_line(barrier)
    pl.semaphore_signal(
        barrier, inc=1, device_id=(place.grp, place.sibling), device_id_type=MESH
    )

    gate_copy = pltpu.make_async_copy(gates, gates_here, gate_sem)
    gate_copy.start()
    halves = [pl.ds(half * HALF, HALF) for half in range(2)]
    x_copies = [
        pltpu.make_async_copy(x.at[levels], x_here.at[levels], x_sem.at[half])
        for half, levels in enumerate(halves)
    ]
    for copy in x_copies:
        copy.start()

    pair_copy.wait()
    base = sign_of(iota((GATE, GATE), 0) * 256 + iota((GATE, GATE), 1), pairs, 0)
    rows = iota((GATE, 128), 0) * 256
    row_sign[...] = sign_of((iota((GATE, 128), 1) % 8) * 65536 + rows, pairs, 0) * sign_of(rows, pairs, 0)
    level = iota((8, GATE), 0) * 65536
    column = iota((8, GATE), 1)
    col_sign = (
        sign_of(level + column, pairs, 0) * sign_of(column, pairs, 0) * sign_of(level, pairs, 0)
    )

    gate_copy.wait()
    middle, last = split_gate(gates_here[0, 0]), split_gate(gates_here[0, 1])

    def layer_one(half):
        x_copies[half].wait()
        for h in range(half * HALF, half * HALF + HALF):
            signed = x_here[h] * base * row_sign[:, h : h + 1] * col_sign[h : h + 1, :]
            state[h] = by_middle(middle, by_last(signed, last))

    def pack_body(block, carry):
        pack_block(place, 0, block, state, tiles_one)
        return carry

    def send_body(number, carry):
        send_block(
            place, 0, BLOCKS - 1 - number, tiles_one, got_one, send_sem.at[0], recv_one
        )
        return carry

    layer_one(0)
    pl.semaphore_wait(barrier, 31 + 7 + 1)
    tell_line(ready)
    lax.fori_loop(0, BLOCKS, pack_body, 0)
    layer_one(1)
    pl.semaphore_wait(ready, 7)
    lax.fori_loop(0, BLOCKS, send_body, 0)
    keep_own(place, 0, tiles_one, got_one, recv_one)
    send_half(place, 1, state, tiles_one, got_one, send_sem.at[0], recv_one)

    for number, (layer, which) in enumerate(((1, 0), (1, 1), (2, 0), (2, 1))):
        wide[number] = split_gate(gates_here[layer, which])
    lane = iota((8, 128), 1)
    levels, row = (lane // 16) % 4 * 65536, iota((8, 128), 0)
    column = place.grp * 16 + lane % 16
    both = (place.dev // 2) * 2 + (place.core + lane // 64) % 2
    arrives = levels + (both * 8 + row) * 256 + column
    leaves = levels + (place.dev * 8 + row) * 256 + column
    sign_one = [sign_of(arrives + half * HALF * 65536, pairs, 1) for half in range(2)]
    sign_two = [sign_of(leaves + half * HALF * 65536, pairs, 2) for half in range(2)]

    for half in range(2):
        take_half(
            place, half, got_one, other, half * HALF, wide.at[1], mine, away_one, come_one,
            recv_one, away_sem.at[0], come_sem_one, sign_one[half],
        )
        for h in range(half * HALF, half * HALF + HALF):
            state[h] = by_middle(wide[0], other[h])
        send_half(
            place, half, state, tiles_two, got_two, send_sem.at[1], recv_two, sign_two[half],
            near_last=half == 1,
        )
    for half, target in enumerate((first, second)):
        take_half(
            place, half, got_two, other, half * HALF, wide.at[3], mine, away_two, come_two,
            recv_two, away_sem.at[1], come_sem_two,
        )
        for h in range(HALF):
            target[h] = by_middle(wide[2], other[half * HALF + h])

    most = pl.ds(0, CHIPS - 1)
    for number, (tiles, away) in enumerate(((tiles_one, away_one), (tiles_two, away_two))):
        for half in range(2):
            part = tiles.at[half, most]
            pltpu.make_async_copy(part, part, send_sem.at[number]).wait()
        pltpu.make_async_copy(away, away, away_sem.at[number]).wait()


def leave_kernel(first, second, out, out_sem):
    copies = []
    for number, part in enumerate((first, second)):
        for piece in range(2):
            here = pl.ds(piece * 2, 2)
            there = pl.ds(number * HALF + piece * 2, 2)
            copies.append(
                pltpu.make_async_copy(part.at[here], out.at[there], out_sem.at[number * 2 + piece])
            )
            copies[-1].start()
    for copy in copies:
        copy.wait()


VMEM = pl.BlockSpec(memory_space=pltpu.VMEM)
ANY = pl.BlockSpec(memory_space=pl.ANY)
STATE = jax.ShapeDtypeStruct((HIGH, GATE, GATE), jnp.float32)
PART = jax.ShapeDtypeStruct((HALF, GATE, GATE), jnp.float32)


def per_device(amplitudes, joined_gates, pair_qubits):
    state = amplitudes.reshape(HIGH, GATE, GATE)
    held = pltpu.VMEM((HIGH, GATE, GATE), jnp.float32)
    tiles = pltpu.VMEM((2, CHIPS, 8, 128), jnp.float32)
    within = pltpu.VMEM((2 * BLOCKS, 128, GATE), jnp.float32)
    dma = pltpu.SemaphoreType.DMA
    first, second = pl.pallas_call(
        window_kernel,
        out_shape=(PART, PART),
        in_specs=[ANY, ANY, ANY],
        out_specs=(VMEM, VMEM),
        scratch_shapes=[
            pltpu.SMEM((3, 2, 8), jnp.int32),
            held,
            pltpu.VMEM((3, 2, GATE, GATE), jnp.float32),
            pltpu.VMEM((4, GATE, 3 * GATE), jnp.bfloat16),
            held,
            held,
            pltpu.VMEM((128, GATE), jnp.float32),
            pltpu.VMEM((GATE, 128), jnp.float32),
            tiles,
            tiles,
            tiles,
            tiles,
            within,
            within,
            within,
            within,
            dma,
            dma((2,)),
            dma,
            dma((2,)),
            dma((2 * BLOCKS,)),
            dma((2 * BLOCKS,)),
            dma((2,)),
            dma((2 * BLOCKS,)),
            dma((2 * BLOCKS,)),
            pltpu.SemaphoreType.REGULAR,
        ],
        name="window",
        compiler_params=pltpu.CompilerParams(
            collective_id=0, has_side_effects=True, vmem_limit_bytes=51 * 2**20
        ),
        cost_estimate=pl.CostEstimate(flops=5 * 2**29, bytes_accessed=2**23, transcendentals=0),
    )(pair_qubits.transpose(0, 2, 1), joined_gates, state)
    out = pl.pallas_call(
        leave_kernel,
        out_shape=STATE,
        in_specs=[VMEM, VMEM],
        out_specs=ANY,
        scratch_shapes=[dma((4,))],
        name="leave",
        compiler_params=pltpu.CompilerParams(vmem_limit_bytes=51 * 2**20),
    )(first, second)
    return out.reshape(amplitudes.shape)


def solution(mesh):
    placed = (P("grp", "dev", None, None, None), P(), P())
    return jax.shard_map(
        per_device,
        mesh=mesh,
        in_specs=placed,
        out_specs=P("grp", "dev", None, None, None),
        check_vma=False,
    )
```
